256 devices in a mesh: rep: 8 (over z), own: 32 (over x, y, core).
Axes of the slice: x: 4, y: 4, z: 8, core: 2. Of those that a mesh axis runs over, the one named last changes fastest.
Arguments:
- grads: bfloat16 [8, 192, 512, 512], P('rep', None, 'own'), may hold values from -6 to 6
- slot_of: int32 [192], P('rep'), may hold values from 0 to 31, as said below
- left_stats: float32 [8, 32, 512, 512], P('rep', 'own'), may hold values from -6 to 6
- right_stats: float32 [8, 32, 512, 512], P('rep', 'own'), may hold values from -6 to 6
- left_roots: bfloat16 [8, 32, 512, 512], P('rep', 'own'), may hold values from -0.25 to 0.25
- right_roots: bfloat16 [8, 32, 512, 512], P('rep', 'own'), may hold values from -0.25 to 0.25
Outputs:
- left_new: float32 [8, 32, 512, 512], P('rep', 'own')
- right_new: float32 [8, 32, 512, 512], P('rep', 'own')
- update: float32 [192, 512, 512], P('rep', 'own')
The draws below stay inside these ranges and needn't reach their ends.
Inputs may be any that keep to these rules, and one draw needn't show every extreme that they name: `slot_of`: within each aligned run of 24 blocks (one group) the values are distinct; the value is the index along `own` of the device that keeps the block's statistics (each owner keeps exactly one slot); in every group 32 - 24 slots hold no block.
All inputs are finite; a program needn't handle non-finite values.
Results may differ from the reference program's by a relative error of at most 0.02.
Values may be sent and summed in bfloat16 or wider, within the bound.
No kernel may reach another device: no remote copies, remote signals or barrier semaphores. Data moves between devices by JAX's collectives and lax.ppermute only.
A program may use at most 128 MiB of HBM per device.

```python
import jax
import jax.numpy as jnp
from jax import lax

BLOCK = 512
GROUP_BLOCKS = 24
BLOCKS = 192
SLOTS = 32
N_REP = 8


def draw_slot_of(key, part):
    key = jax.random.fold_in(key, 7)
    groups = BLOCKS // GROUP_BLOCKS

    def one_group(group_key, group_index):
        shuffled = jax.random.permutation(group_key, SLOTS)
        drawn = shuffled[:GROUP_BLOCKS]
        middle = jax.random.permutation(jax.random.fold_in(group_key, 1), SLOTS - 2) + 1
        forced = jnp.concatenate([jnp.array([0, SLOTS - 1], jnp.int32), middle[:GROUP_BLOCKS - 2].astype(jnp.int32)])
        forced = jax.random.permutation(jax.random.fold_in(group_key, 2), forced)
        return jnp.where(group_index == 0, forced, drawn.astype(jnp.int32))
    keys = jax.random.split(key, groups)
    return jax.vmap(one_group)(keys, jnp.arange(groups)).reshape(-1).astype(jnp.int32)


def strengthened(result, key, source, target, blocks, factor):
    def block_of(position):
        return (jnp.arange(result.shape[position]) // (result.shape[position] // blocks)).reshape((-1,) + (1,) * (result.ndim - 1 - position))

    first = jax.random.permutation(key, blocks)[block_of(target)]
    other_side = (block_of(target) + blocks // 2) % blocks
    return jnp.where((block_of(source) == first) | (block_of(source) == other_side), factor * result, result)


def levels(stream_key, dims, shards, smallest, high):
    level, own = 1.0, jax.random.fold_in(stream_key, 6)
    for position, blocks in shards:
        steps = jnp.exp(jax.random.uniform(jax.random.fold_in(own, position), (blocks,), jnp.float32, smallest / len(shards), high / len(shards)))
        level = level * jnp.repeat(steps, dims[position] // blocks).reshape([-1 if axis == position else 1 for axis in range(len(dims))])
    return level


def bell_draw(key, dims, spread, bound, shards=(), kind=jnp.bfloat16):
    values = spread * jax.random.normal(key, dims, jnp.float32)
    if shards:
        values = values * levels(key, dims, shards, -0.22, 0.18)
    return jnp.clip(values, -bound, bound).astype(kind)


def noise_with(own_key, shape, deviation, limit, pieces, heavy, dtype=jnp.bfloat16):
    values = deviation * jax.random.normal(own_key, shape, jnp.float32)
    if pieces:
        values = values * levels(own_key, shape, pieces, -0.22, 0.18)
    return jnp.clip(strengthened(values, jax.random.fold_in(own_key, 3), *heavy), -limit, limit).astype(dtype)


def setup_inputs(seed: int = 0) -> dict:
    streams_of = jax.random.split(jax.random.key(seed), 7)
    return {
        "grads": noise_with(streams_of[0], (N_REP, BLOCKS, BLOCK, BLOCK), 0.35, 6.0, ((0, 8), (2, 32)), (0, 1, 8, 2.0)),
        "slot_of": draw_slot_of(jax.random.fold_in(streams_of[6], 71), 0),
        "left_stats": bell_draw(streams_of[2], (N_REP, SLOTS, BLOCK, BLOCK), 1.0, 6.0, ((0, 8), (1, 32)), jnp.float32),
        "right_stats": bell_draw(streams_of[3], (N_REP, SLOTS, BLOCK, BLOCK), 1.0, 6.0, ((0, 8), (1, 32)), jnp.float32),
        "left_roots": bell_draw(streams_of[4], (N_REP, SLOTS, BLOCK, BLOCK), BLOCK ** -0.5, 0.25, ((0, 8), (1, 32))),
        "right_roots": bell_draw(streams_of[5], (N_REP, SLOTS, BLOCK, BLOCK), BLOCK ** -0.5, 0.25, ((0, 8), (1, 32))),
    }


DECAY = 0.99
EPSILON = 1e-06

def precondition(block, left, right, left_root, right_root):
    gram_left = jnp.dot(block, block.T, preferred_element_type=jnp.float32)
    gram_right = jnp.dot(block.T, block, preferred_element_type=jnp.float32)
    left_next = DECAY * left + (1.0 - DECAY) * gram_left
    right_next = DECAY * right + (1.0 - DECAY) * gram_right
    half = jnp.dot(left_root, block, preferred_element_type=jnp.float32).astype(jnp.bfloat16)
    precond = jnp.dot(half, right_root, preferred_element_type=jnp.float32)
    wide = block.astype(jnp.float32)
    ratio = jnp.sqrt(jnp.mean(wide * wide) + EPSILON) / jnp.sqrt(jnp.mean(precond * precond) + EPSILON)
    return (left_next, right_next, precond * ratio)

def reference(grads, slot_of, left_stats, right_stats, left_roots, right_roots):
    groups = BLOCKS // GROUP_BLOCKS
    start = jnp.zeros(grads.shape[1:], jnp.float32)
    total = lax.fori_loop(0, grads.shape[0], lambda index, acc: acc + grads[index].astype(jnp.float32), start)
    reduced = total.astype(jnp.bfloat16)
    grouped = reduced.reshape(groups, GROUP_BLOCKS, BLOCK, BLOCK).astype(jnp.float32)
    marks = (slot_of.reshape(groups, GROUP_BLOCKS)[:, :, None] == jnp.arange(SLOTS)[None, None, :]).astype(jnp.float32)
    slotted = jnp.einsum('rgs,rgij->rsij', marks, grouped, precision=lax.Precision.HIGHEST).astype(jnp.bfloat16)
    flat = (slotted.reshape(groups * SLOTS, BLOCK, BLOCK), left_stats.reshape(groups * SLOTS, BLOCK, BLOCK), right_stats.reshape(groups * SLOTS, BLOCK, BLOCK), left_roots.reshape(groups * SLOTS, BLOCK, BLOCK), right_roots.reshape(groups * SLOTS, BLOCK, BLOCK))
    left_next, right_next, grafted = lax.map(lambda items: precondition(*items), flat)
    grafted = grafted.reshape(groups, SLOTS, BLOCK, BLOCK)
    update = jnp.einsum('rgs,rsij->rgij', marks, grafted, precision=lax.Precision.HIGHEST)
    return (left_next.reshape(groups, SLOTS, BLOCK, BLOCK), right_next.reshape(groups, SLOTS, BLOCK, BLOCK), update.reshape(BLOCKS, BLOCK, BLOCK))
```

```python
import jax
import jax.numpy as jnp
from jax import lax
from jax.sharding import PartitionSpec as P

DECAY = 0.99
EPSILON = 1e-06


def reduce_to_group(grads, replicas):
    me = lax.axis_index("rep")
    reach = replicas // 2
    groups = grads.reshape((replicas, -1) + grads.shape[1:])
    cut = groups.shape[1] // 2
    ahead = [(i, (i + 1) % replicas) for i in range(replicas)]
    back = [(i, (i - 1) % replicas) for i in range(replicas)]

    def mine(group):
        return lax.dynamic_index_in_dim(groups, (group + replicas) % replicas, 0, False)

    far = mine(me + reach)
    down = lax.ppermute(far[:cut], "rep", back)
    up = lax.ppermute(far[cut:], "rep", ahead)
    for step in range(reach - 1, 0, -1):
        own_down, own_up = mine(me - step), mine(me + step)
        if step == reach - 1:
            down = jnp.concatenate([own_down[:cut] + down, own_down[cut:]], 0)
            up = jnp.concatenate([own_up[:cut], own_up[cut:] + up], 0)
        else:
            down, up = down + own_down, up + own_up
        down = lax.ppermute(down, "rep", back)
        up = lax.ppermute(up, "rep", ahead)
    wide = down.astype(jnp.float32) + up.astype(jnp.float32) + mine(me).astype(jnp.float32)
    return wide.astype(jnp.bfloat16)


def local(grads, slot_of, left_stats, right_stats, left_roots, right_roots):
    replicas, owners = lax.axis_size("rep"), lax.axis_size("own")
    total = reduce_to_group(grads[0], replicas)
    group, strip, width = total.shape
    block_size = strip * owners

    picks = slot_of[:, None] == jnp.arange(owners)[None, :]
    sends = jnp.einsum(
        "gc,gij->cij", picks.astype(jnp.bfloat16), total, preferred_element_type=jnp.float32
    ).astype(jnp.bfloat16)
    block = lax.all_to_all(sends, "own", 0, 0, tiled=True).reshape(block_size, width)

    half = jnp.dot(left_roots[0, 0], block, preferred_element_type=jnp.float32)
    precond = jnp.dot(
        half.astype(jnp.bfloat16), right_roots[0, 0], preferred_element_type=jnp.float32
    )
    wide = block.astype(jnp.float32)
    ratio = jnp.sqrt(jnp.mean(wide * wide) + EPSILON) / jnp.sqrt(
        jnp.mean(precond * precond) + EPSILON
    )
    grafted = (precond * ratio).astype(jnp.bfloat16).reshape(owners, strip, width)
    rows = lax.all_to_all(grafted, "own", 0, 0, tiled=True)

    gram_left = jnp.einsum("ik,jk->ij", block, block, preferred_element_type=jnp.float32)
    gram_right = jnp.einsum("ki,kj->ij", block, block, preferred_element_type=jnp.float32)
    left_next = DECAY * left_stats[0, 0] + (1.0 - DECAY) * gram_left
    right_next = DECAY * right_stats[0, 0] + (1.0 - DECAY) * gram_right

    update = jnp.einsum(
        "gc,cij->gij", picks.astype(jnp.bfloat16), rows, preferred_element_type=jnp.float32
    )
    return left_next[None, None], right_next[None, None], update


def solution(mesh):
    return jax.shard_map(
        local,
        mesh=mesh,
        in_specs=(
            P("rep", None, "own", None),
            P("rep"),
            P("rep", "own", None, None),
            P("rep", "own", None, None),
            P("rep", "own", None, None),
            P("rep", "own", None, None),
        ),
        out_specs=(P("rep", "own", None, None), P("rep", "own", None, None), P("rep", "own", None)),
        check_vma=False,
    )
```

```python
import functools

import jax
import jax.numpy as jnp
from jax import lax
from jax.experimental import pallas as pl
from jax.experimental.pallas import tpu as pltpu
from jax.sharding import PartitionSpec as P

DECAY = 0.99
EPSILON = 1e-06
PARTS = 2
WAIT_BYTES = 20_000_000
VMEM = pl.BlockSpec(memory_space=pltpu.VMEM)
SMEM = pl.BlockSpec(memory_space=pltpu.SMEM)


def near(array):
    return pltpu.with_memory_space_constraint(array, pltpu.VMEM)


def ordered(first, second):
    return lax.optimization_barrier((first, second))


def add_kernel(got_ref, own_ref, out_ref, *, first, part):
    width = out_ref.shape[2]
    columns = pl.ds(part * width, width)
    blocks, got = out_ref.shape[0], got_ref.shape[0]
    if first > 0:
        out_ref[pl.ds(0, first)] = own_ref[pl.ds(0, first), :, columns]
    rows = pl.ds(first, got)
    out_ref[rows] = got_ref[...] + own_ref[rows, :, columns]
    rest = blocks - first - got
    if rest > 0:
        rows = pl.ds(first + got, rest)
        out_ref[rows] = own_ref[rows, :, columns]


def add(got, own, first, part):
    shape = own.shape[:2] + got.shape[2:]
    return pl.pallas_call(
        functools.partial(add_kernel, first=first, part=part),
        out_shape=jax.ShapeDtypeStruct(shape, got.dtype),
        in_specs=[VMEM] * 2,
        out_specs=VMEM,
        compiler_params=pltpu.CompilerParams(vmem_limit_bytes=4 << 20),
        cost_estimate=pl.CostEstimate(flops=0, bytes_accessed=WAIT_BYTES, transcendentals=0),
        name="add",
    )(near(got), near(own))


def chains(grads, replicas):
    me = lax.axis_index("rep")
    reach = replicas // 2
    groups = grads.reshape((replicas, -1) + grads.shape[1:])
    cut = groups.shape[1] // 2
    width = groups.shape[3] // PARTS
    ahead = [(i, (i + 1) % replicas) for i in range(replicas)]
    back = [(i, (i - 1) % replicas) for i in range(replicas)]

    def mine(group):
        return lax.dynamic_index_in_dim(groups, (group + replicas) % replicas, 0, False)

    def part_of(array, part):
        return array[:, :, part * width : (part + 1) * width]

    downs, ups = [None] * PARTS, [None] * PARTS
    far = mine(me + reach)
    for part in range(PARTS):
        downs[part] = lax.ppermute(part_of(far[:cut], part), "rep", back)
        ups[part] = lax.ppermute(part_of(far[cut:], part), "rep", ahead)
    last = None
    for step in range(reach - 1, 0, -1):
        own_down, own_up = mine(me - step), mine(me + step)
        start = cut if step == reach - 1 else 0
        for part in range(PARTS):
            down, up = downs[part], ups[part]
            if last is not None:
                last, down = ordered(last, down)
            down = add(down, own_down, 0, part)
            downs[part] = lax.ppermute(down, "rep", back)
            down, up = ordered(down, up)
            last = up = add(up, own_up, start, part)
            ups[part] = lax.ppermute(up, "rep", ahead)
    return downs, ups, mine(me)


def widen_kernel(own_ref, down_ref, out_ref, *, part):
    width = out_ref.shape[2]
    columns = pl.ds(part * width, width)
    out_ref[...] = down_ref[...].astype(jnp.float32) + own_ref[:, :, columns].astype(jnp.float32)


def widen(own, down, part):
    return pl.pallas_call(
        functools.partial(widen_kernel, part=part),
        out_shape=jax.ShapeDtypeStruct(down.shape, jnp.float32),
        in_specs=[VMEM] * 2,
        out_specs=VMEM,
        compiler_params=pltpu.CompilerParams(vmem_limit_bytes=4 << 20),
        cost_estimate=pl.CostEstimate(flops=0, bytes_accessed=WAIT_BYTES, transcendentals=0),
        name="widen",
    )(near(own), near(down))


def place_kernel(slot_ref, wide_ref, up_ref, *refs):
    before, out_ref = refs[:-1], refs[-1]
    width = up_ref.shape[2]
    here = pl.ds(out_ref.shape[2] - width, width)
    out_ref[:, :, here] = jnp.zeros((out_ref.shape[0],) + up_ref.shape[1:], out_ref.dtype)
    for ref in before:
        out_ref[:, :, pl.ds(0, ref.shape[2])] = ref[...]
    for b in range(up_ref.shape[0]):
        total = wide_ref[b] + up_ref[b].astype(jnp.float32)
        out_ref[slot_ref[b], :, here] = total.astype(out_ref.dtype)


def place(slot_of, wide, up, before, owners):
    strip, width = up.shape[1:]
    earlier = [] if before is None else [before]
    columns = width + sum(a.shape[2] for a in earlier)
    return pl.pallas_call(
        place_kernel,
        out_shape=jax.ShapeDtypeStruct((owners, strip, columns), up.dtype),
        in_specs=[SMEM] + [VMEM] * (2 + len(earlier)),
        out_specs=VMEM,
        compiler_params=pltpu.CompilerParams(vmem_limit_bytes=8 << 20),
        cost_estimate=pl.CostEstimate(flops=0, bytes_accessed=WAIT_BYTES, transcendentals=0),
        name="place",
    )(slot_of, near(wide), near(up), *[near(a) for a in earlier])


def step_kernel(block_ref, left_ref, right_ref, out_ref, precond_ref):
    size = block_ref.shape[0]
    tile = size // 4
    block = block_ref[...]
    squares = jnp.zeros((tile, size), jnp.float32)
    inputs = jnp.zeros((tile, size), jnp.float32)
    for i in range(4):
        rows = pl.ds(i * tile, tile)
        wide = block_ref[rows, :].astype(jnp.float32)
        inputs += wide * wide
        half = jnp.dot(left_ref[rows, :], block, preferred_element_type=jnp.float32)
        precond = jnp.dot(
            half.astype(jnp.bfloat16), right_ref[...], preferred_element_type=jnp.float32
        )
        precond_ref[rows, :] = precond
        squares += precond * precond
    count = 1.0 / (size * size)
    ratio = jnp.sqrt(jnp.sum(inputs, keepdims=True) * count + EPSILON) / jnp.sqrt(
        jnp.sum(squares, keepdims=True) * count + EPSILON
    )
    for i in range(4):
        rows = pl.ds(i * tile, tile)
        out_ref[rows, :] = (precond_ref[rows, :] * ratio).astype(out_ref.dtype)


def graft(block, left_root, right_root):
    size = block.shape[0]
    return pl.pallas_call(
        step_kernel,
        out_shape=jax.ShapeDtypeStruct(block.shape, block.dtype),
        in_specs=[VMEM] * 3,
        out_specs=VMEM,
        scratch_shapes=[pltpu.VMEM(block.shape, jnp.float32)],
        compiler_params=pltpu.CompilerParams(vmem_limit_bytes=8 << 20),
        cost_estimate=pl.CostEstimate(
            flops=4 * size**3, bytes_accessed=4 * block.size * 2, transcendentals=0
        ),
        name="graft",
    )(near(block), near(left_root), near(right_root))


def pick_kernel(slot_ref, rows_ref, out_ref):
    for b in range(out_ref.shape[0]):
        out_ref[b] = rows_ref[slot_ref[b]].astype(out_ref.dtype)


def pick(slot_of, rows):
    return pl.pallas_call(
        pick_kernel,
        out_shape=jax.ShapeDtypeStruct(slot_of.shape + rows.shape[1:], jnp.float32),
        in_specs=[SMEM, VMEM],
        out_specs=VMEM,
        compiler_params=pltpu.CompilerParams(vmem_limit_bytes=8 << 20),
        cost_estimate=pl.CostEstimate(flops=0, bytes_accessed=1_300_000, transcendentals=0),
        name="pick",
    )(slot_of, near(rows))


def local(grads, slot_of, left_stats, right_stats, left_roots, right_roots):
    replicas, owners = lax.axis_size("rep"), lax.axis_size("own")
    downs, ups, own = chains(grads[0], replicas)
    strip, width = own.shape[1:]
    block_size = strip * owners

    sends = None
    for part in range(PARTS):
        down, up = downs[part], ups[part]
        if sends is not None:
            sends, down = ordered(sends, down)
        wide = widen(own, down, part)
        wide, up = ordered(wide, up)
        sends = place(slot_of, wide, up, sends, owners)
    block = lax.all_to_all(sends, "own", 0, 0, tiled=True).reshape(block_size, width)

    grafted = graft(block, left_roots[0, 0], right_roots[0, 0]).reshape(owners, strip, width)
    rows = lax.all_to_all(grafted, "own", 0, 0, tiled=True)

    gram_left = jnp.einsum("ik,jk->ij", block, block, preferred_element_type=jnp.float32)
    gram_right = jnp.einsum("ki,kj->ij", block, block, preferred_element_type=jnp.float32)
    left_next = DECAY * left_stats[0, 0] + (1.0 - DECAY) * gram_left
    right_next = DECAY * right_stats[0, 0] + (1.0 - DECAY) * gram_right

    update = pick(slot_of, rows)
    return left_next[None, None], right_next[None, None], update


def solution(mesh):
    return jax.shard_map(
        local,
        mesh=mesh,
        in_specs=(
            P("rep", None, "own", None),
            P("rep"),
            P("rep", "own", None, None),
            P("rep", "own", None, None),
            P("rep", "own", None, None),
            P("rep", "own", None, None),
        ),
        out_specs=(P("rep", "own", None, None), P("rep", "own", None, None), P("rep", "own", None)),
        check_vma=False,
    )
```

```python
import functools

import jax
import jax.numpy as jnp
from jax import lax
from jax.experimental import pallas as pl
from jax.experimental.pallas import tpu as pltpu
from jax.sharding import PartitionSpec as P

DECAY = 0.99
EPSILON = 1e-06
PARTS = 2
WAIT_BYTES = 20_000_000
VMEM = pl.BlockSpec(memory_space=pltpu.VMEM)
SMEM = pl.BlockSpec(memory_space=pltpu.SMEM)


def near(array):
    return pltpu.with_memory_space_constraint(array, pltpu.VMEM)


def ordered(first, second):
    return lax.optimization_barrier((first, second))


def add_kernel(got_ref, own_ref, out_ref, *, first, part):
    width = out_ref.shape[2]
    columns = pl.ds(part * width, width)
    blocks, got = out_ref.shape[0], got_ref.shape[0]
    if first > 0:
        out_ref[pl.ds(0, first)] = own_ref[pl.ds(0, first), :, columns]
    rows = pl.ds(first, got)
    out_ref[rows] = got_ref[...] + own_ref[rows, :, columns]
    rest = blocks - first - got
    if rest > 0:
        rows = pl.ds(first + got, rest)
        out_ref[rows] = own_ref[rows, :, columns]


def add(got, own, first, part):
    shape = own.shape[:2] + got.shape[2:]
    return pl.pallas_call(
        functools.partial(add_kernel, first=first, part=part),
        out_shape=jax.ShapeDtypeStruct(shape, got.dtype),
        in_specs=[VMEM] * 2,
        out_specs=VMEM,
        compiler_params=pltpu.CompilerParams(vmem_limit_bytes=4 << 20),
        cost_estimate=pl.CostEstimate(flops=0, bytes_accessed=WAIT_BYTES, transcendentals=0),
        name="add",
    )(near(got), near(own))


def chains(grads, replicas):
    me = lax.axis_index("rep")
    reach = replicas // 2
    groups = grads.reshape((replicas, -1) + grads.shape[1:])
    width = groups.shape[3] // PARTS
    ahead = [(i, (i + 1) % replicas) for i in range(replicas)]
    back = [(i, (i - 1) % replicas) for i in range(replicas)]

    def mine(group):
        return lax.dynamic_index_in_dim(groups, (group + replicas) % replicas, 0, False)

    def part_of(array, part):
        return array[:, :, part * width : (part + 1) * width]

    far, below, above = mine(me + reach), mine(me - reach + 1), mine(me + reach - 1)
    down = [lax.ppermute(part_of(far, 0), "rep", back), None]
    up = [None, lax.ppermute(part_of(far, 1), "rep", ahead)]
    down[1] = lax.ppermute(part_of(below, 1), "rep", back)
    up[0] = lax.ppermute(part_of(above, 0), "rep", ahead)
    last = None
    for step in range(reach - 1, 0, -1):
        for at, one, two in ((step, 0, 1), (step - 1, 1, 0)):
            if at == 0:
                continue
            for array, part, group, pairs in (
                (down, one, me - at, back),
                (up, two, me + at, ahead),
            ):
                got = array[part]
                if last is not None:
                    last, got = ordered(last, got)
                last = add(got, mine(group), 0, part)
                array[part] = lax.ppermute(last, "rep", pairs)
    return down, up, mine(me), last


def widen_kernel(own_ref, down_ref, out_ref, *, part):
    width = out_ref.shape[2]
    columns = pl.ds(part * width, width)
    out_ref[...] = down_ref[...].astype(jnp.float32) + own_ref[:, :, columns].astype(jnp.float32)


def widen(own, down, part):
    return pl.pallas_call(
        functools.partial(widen_kernel, part=part),
        out_shape=jax.ShapeDtypeStruct(down.shape, jnp.float32),
        in_specs=[VMEM] * 2,
        out_specs=VMEM,
        compiler_params=pltpu.CompilerParams(vmem_limit_bytes=4 << 20),
        cost_estimate=pl.CostEstimate(flops=0, bytes_accessed=WAIT_BYTES, transcendentals=0),
        name="widen",
    )(near(own), near(down))


def place_kernel(slot_ref, wide_ref, up_ref, *refs):
    before, out_ref = refs[:-1], refs[-1]
    width = up_ref.shape[2]
    here = pl.ds(out_ref.shape[2] - width, width)
    out_ref[:, :, here] = jnp.zeros((out_ref.shape[0],) + up_ref.shape[1:], out_ref.dtype)
    for ref in before:
        out_ref[:, :, pl.ds(0, ref.shape[2])] = ref[...]
    for b in range(up_ref.shape[0]):
        total = wide_ref[b] + up_ref[b].astype(jnp.float32)
        out_ref[slot_ref[b], :, here] = total.astype(out_ref.dtype)


def place(slot_of, wide, up, before, owners):
    strip, width = up.shape[1:]
    earlier = [] if before is None else [before]
    columns = width + sum(a.shape[2] for a in earlier)
    return pl.pallas_call(
        place_kernel,
        out_shape=jax.ShapeDtypeStruct((owners, strip, columns), up.dtype),
        in_specs=[SMEM] + [VMEM] * (2 + len(earlier)),
        out_specs=VMEM,
        compiler_params=pltpu.CompilerParams(vmem_limit_bytes=8 << 20),
        cost_estimate=pl.CostEstimate(flops=0, bytes_accessed=WAIT_BYTES, transcendentals=0),
        name="place",
    )(slot_of, near(wide), near(up), *[near(a) for a in earlier])


def step_kernel(block_ref, left_ref, right_ref, out_ref, precond_ref):
    size = block_ref.shape[0]
    tile = size // 4
    block = block_ref[...]
    squares = jnp.zeros((tile, size), jnp.float32)
    inputs = jnp.zeros((tile, size), jnp.float32)
    for i in range(4):
        rows = pl.ds(i * tile, tile)
        wide = block_ref[rows, :].astype(jnp.float32)
        inputs += wide * wide
        half = jnp.dot(left_ref[rows, :], block, preferred_element_type=jnp.float32)
        precond = jnp.dot(
            half.astype(jnp.bfloat16), right_ref[...], preferred_element_type=jnp.float32
        )
        precond_ref[rows, :] = precond
        squares += precond * precond
    count = 1.0 / (size * size)
    ratio = jnp.sqrt(jnp.sum(inputs, keepdims=True) * count + EPSILON) / jnp.sqrt(
        jnp.sum(squares, keepdims=True) * count + EPSILON
    )
    for i in range(4):
        rows = pl.ds(i * tile, tile)
        out_ref[rows, :] = (precond_ref[rows, :] * ratio).astype(out_ref.dtype)


def graft(block, left_root, right_root):
    size = block.shape[0]
    return pl.pallas_call(
        step_kernel,
        out_shape=jax.ShapeDtypeStruct(block.shape, block.dtype),
        in_specs=[VMEM] * 3,
        out_specs=VMEM,
        scratch_shapes=[pltpu.VMEM(block.shape, jnp.float32)],
        compiler_params=pltpu.CompilerParams(vmem_limit_bytes=8 << 20),
        cost_estimate=pl.CostEstimate(
            flops=4 * size**3, bytes_accessed=4 * block.size * 2, transcendentals=0
        ),
        name="graft",
    )(near(block), near(left_root), near(right_root))


def pick_kernel(slot_ref, rows_ref, out_ref):
    for b in range(out_ref.shape[0]):
        out_ref[b] = rows_ref[slot_ref[b]].astype(out_ref.dtype)


def pick(slot_of, rows):
    return pl.pallas_call(
        pick_kernel,
        out_shape=jax.ShapeDtypeStruct(slot_of.shape + rows.shape[1:], jnp.float32),
        in_specs=[SMEM, VMEM],
        out_specs=VMEM,
        compiler_params=pltpu.CompilerParams(vmem_limit_bytes=8 << 20),
        cost_estimate=pl.CostEstimate(flops=0, bytes_accessed=1_300_000, transcendentals=0),
        name="pick",
    )(slot_of, near(rows))


def local(grads, slot_of, left_stats, right_stats, left_roots, right_roots):
    replicas, owners = lax.axis_size("rep"), lax.axis_size("own")
    downs, ups, own, last = chains(grads[0], replicas)
    strip, width = own.shape[1:]
    block_size = strip * owners

    near_down, near_up = downs[1], ups[0]
    last, near_down = ordered(last, near_down)
    wide_last = widen(own, near_down, 1)
    wide_last, near_up = ordered(wide_last, near_up)
    wide_first = widen(own, near_up, 0)
    wide_first, far_down = ordered(wide_first, downs[0])
    sends = place(slot_of, wide_first, far_down, None, owners)
    sends, far_up = ordered(sends, ups[1])
    sends = place(slot_of, wide_last, far_up, sends, owners)
    block = lax.all_to_all(sends, "own", 0, 0, tiled=True).reshape(block_size, width)

    grafted = graft(block, left_roots[0, 0], right_roots[0, 0]).reshape(owners, strip, width)
    rows = lax.all_to_all(grafted, "own", 0, 0, tiled=True)

    gram_left = jnp.einsum("ik,jk->ij", block, block, preferred_element_type=jnp.float32)
    gram_right = jnp.einsum("ki,kj->ij", block, block, preferred_element_type=jnp.float32)
    left_next = DECAY * left_stats[0, 0] + (1.0 - DECAY) * gram_left
    right_next = DECAY * right_stats[0, 0] + (1.0 - DECAY) * gram_right

    update = pick(slot_of, rows)
    return left_next[None, None], right_next[None, None], update


def solution(mesh):
    return jax.shard_map(
        local,
        mesh=mesh,
        in_specs=(
            P("rep", None, "own", None),
            P("rep"),
            P("rep", "own", None, None),
            P("rep", "own", None, None),
            P("rep", "own", None, None),
            P("rep", "own", None, None),
        ),
        out_specs=(P("rep", "own", None, None), P("rep", "own", None, None), P("rep", "own", None)),
        check_vma=False,
    )
```

```python
import functools

import jax
import jax.numpy as jnp
from jax import lax
from jax.experimental import pallas as pl
from jax.experimental.pallas import tpu as pltpu
from jax.sharding import PartitionSpec as P

DECAY = 0.99
EPSILON = 1e-06
PARTS = 2
WAIT_BYTES = 20_000_000
VMEM = pl.BlockSpec(memory_space=pltpu.VMEM)
SMEM = pl.BlockSpec(memory_space=pltpu.SMEM)


def near(array):
    return pltpu.with_memory_space_constraint(array, pltpu.VMEM)


def ordered(first, second):
    return lax.optimization_barrier((first, second))


def add_kernel(got_ref, own_ref, out_ref, *, first, part):
    width = out_ref.shape[2]
    columns = pl.ds(part * width, width)
    blocks, got = out_ref.shape[0], got_ref.shape[0]
    if first > 0:
        out_ref[pl.ds(0, first)] = own_ref[pl.ds(0, first), :, columns]
    rows = pl.ds(first, got)
    out_ref[rows] = got_ref[...] + own_ref[rows, :, columns]
    rest = blocks - first - got
    if rest > 0:
        rows = pl.ds(first + got, rest)
        out_ref[rows] = own_ref[rows, :, columns]


def add(got, own, first, part):
    shape = own.shape[:2] + got.shape[2:]
    return pl.pallas_call(
        functools.partial(add_kernel, first=first, part=part),
        out_shape=jax.ShapeDtypeStruct(shape, got.dtype),
        in_specs=[VMEM] * 2,
        out_specs=VMEM,
        compiler_params=pltpu.CompilerParams(vmem_limit_bytes=4 << 20),
        cost_estimate=pl.CostEstimate(flops=0, bytes_accessed=WAIT_BYTES, transcendentals=0),
        name="add",
    )(near(got), near(own))


def chains(grads, replicas):
    me = lax.axis_index("rep")
    reach = replicas // 2
    groups = grads.reshape((replicas, -1) + grads.shape[1:])
    width = groups.shape[3] // PARTS
    ahead = [(i, (i + 1) % replicas) for i in range(replicas)]
    back = [(i, (i - 1) % replicas) for i in range(replicas)]

    def mine(group):
        return lax.dynamic_index_in_dim(groups, (group + replicas) % replicas, 0, False)

    def part_of(array, part):
        return array[:, :, part * width : (part + 1) * width]

    far = mine(me + reach)
    far, groups = ordered(far, groups)
    down = [lax.ppermute(part_of(far, 0), "rep", back), None]
    up = [None, lax.ppermute(part_of(far, 1), "rep", ahead)]
    below, above = mine(me - reach + 1), mine(me + reach - 1)
    down[1] = lax.ppermute(part_of(below, 1), "rep", back)
    up[0] = lax.ppermute(part_of(above, 0), "rep", ahead)
    last = None
    for step in range(reach - 1, 0, -1):
        for at, one, two in ((step, 0, 1), (step - 1, 1, 0)):
            if at == 0:
                continue
            for array, part, group, pairs in (
                (down, one, me - at, back),
                (up, two, me + at, ahead),
            ):
                got = array[part]
                if last is not None:
                    last, got = ordered(last, got)
                last = add(got, mine(group), 0, part)
                array[part] = lax.ppermute(last, "rep", pairs)
    return down, up, mine(me), last


def widen_kernel(own_ref, down_ref, out_ref, *, part):
    width = out_ref.shape[2]
    columns = pl.ds(part * width, width)
    out_ref[...] = down_ref[...].astype(jnp.float32) + own_ref[:, :, columns].astype(jnp.float32)


def widen(own, down, part):
    return pl.pallas_call(
        functools.partial(widen_kernel, part=part),
        out_shape=jax.ShapeDtypeStruct(down.shape, jnp.float32),
        in_specs=[VMEM] * 2,
        out_specs=VMEM,
        compiler_params=pltpu.CompilerParams(vmem_limit_bytes=4 << 20),
        cost_estimate=pl.CostEstimate(flops=0, bytes_accessed=WAIT_BYTES, transcendentals=0),
        name="widen",
    )(near(own), near(down))


def narrow_kernel(wide_ref, got_ref, out_ref):
    out_ref[...] = (wide_ref[...] + got_ref[...].astype(jnp.float32)).astype(out_ref.dtype)


def narrow(wide, got):
    return pl.pallas_call(
        narrow_kernel,
        out_shape=jax.ShapeDtypeStruct(got.shape, got.dtype),
        in_specs=[VMEM] * 2,
        out_specs=VMEM,
        compiler_params=pltpu.CompilerParams(vmem_limit_bytes=4 << 20),
        cost_estimate=pl.CostEstimate(flops=0, bytes_accessed=WAIT_BYTES, transcendentals=0),
        name="narrow",
    )(near(wide), near(got))


def place_kernel(slot_ref, first_ref, wide_ref, got_ref, out_ref):
    width = got_ref.shape[2]
    out_ref[...] = jnp.zeros_like(out_ref)
    for b in range(got_ref.shape[0]):
        slot = slot_ref[b]
        total = wide_ref[b] + got_ref[b].astype(jnp.float32)
        out_ref[slot, :, pl.ds(0, width)] = first_ref[b]
        out_ref[slot, :, pl.ds(width, width)] = total.astype(out_ref.dtype)


def place(slot_of, first, wide, got, owners):
    strip, width = got.shape[1:]
    return pl.pallas_call(
        place_kernel,
        out_shape=jax.ShapeDtypeStruct((owners, strip, PARTS * width), got.dtype),
        in_specs=[SMEM] + [VMEM] * 3,
        out_specs=VMEM,
        compiler_params=pltpu.CompilerParams(vmem_limit_bytes=8 << 20),
        cost_estimate=pl.CostEstimate(flops=0, bytes_accessed=WAIT_BYTES, transcendentals=0),
        name="place",
    )(slot_of, near(first), near(wide), near(got))


def step_kernel(block_ref, left_ref, right_ref, out_ref, precond_ref):
    size = block_ref.shape[0]
    tile = size // 2
    block = block_ref[...]
    squares = jnp.zeros((tile, size), jnp.float32)
    inputs = jnp.zeros((tile, size), jnp.float32)
    for i in range(2):
        rows = pl.ds(i * tile, tile)
        wide = block_ref[rows, :].astype(jnp.float32)
        inputs += wide * wide
        half = jnp.dot(left_ref[rows, :], block, preferred_element_type=jnp.float32)
        precond = jnp.dot(
            half.astype(jnp.bfloat16), right_ref[...], preferred_element_type=jnp.float32
        )
        precond_ref[rows, :] = precond
        squares += precond * precond
    count = 1.0 / (size * size)
    ratio = jnp.sqrt(jnp.sum(inputs, keepdims=True) * count + EPSILON) / jnp.sqrt(
        jnp.sum(squares, keepdims=True) * count + EPSILON
    )
    for i in range(2):
        rows = pl.ds(i * tile, tile)
        out_ref[rows, :] = (precond_ref[rows, :] * ratio).astype(out_ref.dtype)


def graft(block, left_root, right_root):
    size = block.shape[0]
    return pl.pallas_call(
        step_kernel,
        out_shape=jax.ShapeDtypeStruct(block.shape, block.dtype),
        in_specs=[VMEM] * 3,
        out_specs=VMEM,
        scratch_shapes=[pltpu.VMEM(block.shape, jnp.float32)],
        compiler_params=pltpu.CompilerParams(vmem_limit_bytes=8 << 20),
        cost_estimate=pl.CostEstimate(
            flops=4 * size**3, bytes_accessed=4 * block.size * 2, transcendentals=0
        ),
        name="graft",
    )(near(block), near(left_root), near(right_root))


def pick_kernel(slot_ref, rows_ref, out_ref, wide_ref, sems):
    chunks = sems.shape[0]
    count = wide_ref.shape[0] // chunks
    copies = []
    for chunk in range(chunks):
        blocks = pl.ds(chunk * count, count)
        for b in range(chunk * count, (chunk + 1) * count):
            wide_ref[b] = rows_ref[slot_ref[b]].astype(wide_ref.dtype)
        copy = pltpu.make_async_copy(wide_ref.at[blocks], out_ref.at[blocks], sems.at[chunk])
        copy.start()
        copies.append(copy)
    for copy in copies:
        copy.wait()


def pick(slot_of, rows):
    shape = slot_of.shape + rows.shape[1:]
    return pl.pallas_call(
        pick_kernel,
        out_shape=jax.ShapeDtypeStruct(shape, jnp.float32),
        in_specs=[SMEM, VMEM],
        out_specs=pl.BlockSpec(memory_space=pl.ANY),
        scratch_shapes=[pltpu.VMEM(shape, jnp.float32), pltpu.SemaphoreType.DMA((4,))],
        compiler_params=pltpu.CompilerParams(vmem_limit_bytes=8 << 20),
        cost_estimate=pl.CostEstimate(flops=0, bytes_accessed=1_300_000, transcendentals=0),
        name="pick",
    )(slot_of, near(rows))


def local(grads, slot_of, left_stats, right_stats, left_roots, right_roots):
    replicas, owners = lax.axis_size("rep"), lax.axis_size("own")
    downs, ups, own, last = chains(grads[0], replicas)
    strip, width = own.shape[1:]
    block_size = strip * owners

    near_down, near_up = downs[1], ups[0]
    last, near_down = ordered(last, near_down)
    wide_last = widen(own, near_down, 1)
    wide_last, near_up = ordered(wide_last, near_up)
    wide_first = widen(own, near_up, 0)
    wide_first, far_down = ordered(wide_first, downs[0])
    first = narrow(wide_first, far_down)
    sends = place(slot_of, first, wide_last, ups[1], owners)
    block = lax.all_to_all(sends, "own", 0, 0, tiled=True).reshape(block_size, width)

    grafted = graft(block, left_roots[0, 0], right_roots[0, 0]).reshape(owners, strip, width)
    rows = lax.all_to_all(grafted, "own", 0, 0, tiled=True)

    gram_left = jnp.einsum("ik,jk->ij", block, block, preferred_element_type=jnp.float32)
    gram_right = jnp.einsum("ki,kj->ij", block, block, preferred_element_type=jnp.float32)
    left_next = DECAY * left_stats[0, 0] + (1.0 - DECAY) * gram_left
    right_next = DECAY * right_stats[0, 0] + (1.0 - DECAY) * gram_right

    update = pick(slot_of, rows)
    return left_next[None, None], right_next[None, None], update


def solution(mesh):
    return jax.shard_map(
        local,
        mesh=mesh,
        in_specs=(
            P("rep", None, "own", None),
            P("rep"),
            P("rep", "own", None, None),
            P("rep", "own", None, None),
            P("rep", "own", None, None),
            P("rep", "own", None, None),
        ),
        out_specs=(P("rep", "own", None, None), P("rep", "own", None, None), P("rep", "own", None)),
        check_vma=False,
    )
```

```python
import functools

import jax
import jax.numpy as jnp
from jax import lax
from jax.experimental import pallas as pl
from jax.experimental.pallas import tpu as pltpu
from jax.sharding import PartitionSpec as P

DECAY = 0.99
EPSILON = 1e-06
PARTS = 2
WAIT_BYTES = 20_000_000
VMEM = pl.BlockSpec(memory_space=pltpu.VMEM)


def near(array):
    return pltpu.with_memory_space_constraint(array, pltpu.VMEM)


def ordered(first, second):
    return lax.optimization_barrier((first, second))


def slice_kernel(groups_ref, one_ref, two_ref, sems, *, picks):
    me = lax.axis_index("rep")
    width = one_ref.shape[2]
    copies = []
    for at, (out_ref, (ahead, part)) in enumerate(zip((one_ref, two_ref), picks)):
        group = lax.rem(me + ahead, groups_ref.shape[0])
        source = groups_ref.at[group, :, :, pl.ds(part * width, width)]
        copies.append(pltpu.make_async_copy(source, out_ref, sems.at[at]))
    for copy in copies:
        copy.start()
    for copy in copies:
        copy.wait()


def slices(groups, picks):
    shape = groups.shape[1:3] + (groups.shape[3] // PARTS,)
    return pl.pallas_call(
        functools.partial(slice_kernel, picks=picks),
        out_shape=[jax.ShapeDtypeStruct(shape, groups.dtype)] * 2,
        in_specs=[pl.BlockSpec(memory_space=pltpu.HBM)],
        out_specs=[VMEM] * 2,
        scratch_shapes=[pltpu.SemaphoreType.DMA((2,))],
        compiler_params=pltpu.CompilerParams(vmem_limit_bytes=4 << 20),
        cost_estimate=pl.CostEstimate(flops=0, bytes_accessed=1_000_000, transcendentals=0),
        name="slices",
    )(pltpu.with_memory_space_constraint(groups, pltpu.HBM))


def add_kernel(got_ref, own_ref, out_ref, *, first, part):
    width = out_ref.shape[2]
    columns = pl.ds(part * width, width)
    blocks, got = out_ref.shape[0], got_ref.shape[0]
    if first > 0:
        out_ref[pl.ds(0, first)] = own_ref[pl.ds(0, first), :, columns]
    rows = pl.ds(first, got)
    out_ref[rows] = got_ref[...] + own_ref[rows, :, columns]
    rest = blocks - first - got
    if rest > 0:
        rows = pl.ds(first + got, rest)
        out_ref[rows] = own_ref[rows, :, columns]


def add(got, own, first, part):
    shape = own.shape[:2] + got.shape[2:]
    return pl.pallas_call(
        functools.partial(add_kernel, first=first, part=part),
        out_shape=jax.ShapeDtypeStruct(shape, got.dtype),
        in_specs=[VMEM] * 2,
        out_specs=VMEM,
        compiler_params=pltpu.CompilerParams(vmem_limit_bytes=4 << 20),
        cost_estimate=pl.CostEstimate(flops=0, bytes_accessed=WAIT_BYTES, transcendentals=0),
        name="add",
    )(near(got), near(own))


def chains(grads, replicas, chosen):
    me = lax.axis_index("rep")
    reach = replicas // 2
    groups = grads.reshape((replicas, -1) + grads.shape[1:])
    ahead = [(i, (i - 1) % replicas) for i in range(replicas)]
    back = [(i, (i + 1) % replicas) for i in range(replicas)]

    def mine(group):
        return lax.dynamic_index_in_dim(groups, (group + replicas) % replicas, 0, False)

    down, up = [None, None], [None, None]
    one, two = slices(groups, ((reach, 0), (reach, 1)))
    down[0], up[1] = lax.ppermute(one, "rep", back), lax.ppermute(two, "rep", ahead)
    one, groups = ordered(one, groups)
    one, two = slices(groups, ((reach - 1, 1), (reach + 1, 0)))
    down[1], up[0] = lax.ppermute(one, "rep", back), lax.ppermute(two, "rep", ahead)
    one, groups = ordered(one, groups)
    last = None
    for step in range(reach - 1, 0, -1):
        for at, one, two in ((step, 0, 1), (step - 1, 1, 0)):
            if at == 0:
                continue
            for array, part, group, pairs in (
                (down, one, me + at, back),
                (up, two, me - at, ahead),
            ):
                got = array[part]
                if last is not None:
                    last, got = ordered(last, got)
                if step == reach - 2 and not at == step:
                    chosen, got = ordered(chosen, got)
                last = add(got, mine(group), 0, part)
                array[part] = lax.ppermute(last, "rep", pairs)
    return down, up, mine(me), last, chosen


def widen_kernel(own_ref, down_ref, out_ref, *, part):
    width = out_ref.shape[2]
    columns = pl.ds(part * width, width)
    out_ref[...] = down_ref[...].astype(jnp.float32) + own_ref[:, :, columns].astype(jnp.float32)


def widen(own, down, part):
    return pl.pallas_call(
        functools.partial(widen_kernel, part=part),
        out_shape=jax.ShapeDtypeStruct(down.shape, jnp.float32),
        in_specs=[VMEM] * 2,
        out_specs=VMEM,
        compiler_params=pltpu.CompilerParams(vmem_limit_bytes=4 << 20),
        cost_estimate=pl.CostEstimate(flops=0, bytes_accessed=WAIT_BYTES, transcendentals=0),
        name="widen",
    )(near(own), near(down))


def selections(slot_of, owners, strip):
    slot = jnp.repeat(slot_of, strip)
    blocks, slots = jnp.arange(slot.shape[0]), jnp.arange(owners * strip)
    same_row = blocks[None, :] % strip == slots[:, None] % strip
    put = (slot[None, :] == slots[:, None] // strip) & same_row
    take = (slot[:, None] == slots[None, :] // strip) & (
        blocks[:, None] % strip == slots[None, :] % strip
    )
    return put.astype(jnp.bfloat16), take.astype(jnp.bfloat16)


def place_kernel(put_ref, wide_ref, got_ref, *refs):
    before, out_ref = refs[:-1], refs[-1]
    width = got_ref.shape[2]
    total = (wide_ref[...] + got_ref[...].astype(jnp.float32)).astype(out_ref.dtype)
    for ref in before:
        out_ref[:, pl.ds(0, ref.shape[1])] = ref[...]
    out_ref[:, pl.ds(out_ref.shape[1] - width, width)] = jnp.dot(
        put_ref[...], total.reshape(-1, width), preferred_element_type=jnp.float32
    ).astype(out_ref.dtype)


def place(put, wide, got, *before):
    width = got.shape[2]
    columns = width + sum(a.shape[1] for a in before)
    return pl.pallas_call(
        place_kernel,
        out_shape=jax.ShapeDtypeStruct((put.shape[0], columns), got.dtype),
        in_specs=[VMEM] * (3 + len(before)),
        out_specs=VMEM,
        compiler_params=pltpu.CompilerParams(vmem_limit_bytes=8 << 20),
        cost_estimate=pl.CostEstimate(flops=0, bytes_accessed=WAIT_BYTES, transcendentals=0),
        name="place",
    )(*[near(a) for a in (put, wide, got) + before])


def step_kernel(block_ref, left_ref, right_ref, out_ref, precond_ref):
    size = block_ref.shape[0]
    tile = size
    block = block_ref[...]
    squares = jnp.zeros((tile, size), jnp.float32)
    inputs = jnp.zeros((tile, size), jnp.float32)
    for i in range(1):
        rows = pl.ds(i * tile, tile)
        wide = block_ref[rows, :].astype(jnp.float32)
        inputs += wide * wide
        half = jnp.dot(left_ref[rows, :], block, preferred_element_type=jnp.float32)
        precond = jnp.dot(
            half.astype(jnp.bfloat16), right_ref[...], preferred_element_type=jnp.float32
        )
        precond_ref[rows, :] = precond
        squares += precond * precond
    count = 1.0 / (size * size)
    ratio = jnp.sqrt(jnp.sum(inputs, keepdims=True) * count + EPSILON) / jnp.sqrt(
        jnp.sum(squares, keepdims=True) * count + EPSILON
    )
    for i in range(1):
        rows = pl.ds(i * tile, tile)
        out_ref[rows, :] = (precond_ref[rows, :] * ratio).astype(out_ref.dtype)


def graft(block, left_root, right_root):
    size = block.shape[0]
    return pl.pallas_call(
        step_kernel,
        out_shape=jax.ShapeDtypeStruct(block.shape, block.dtype),
        in_specs=[VMEM] * 3,
        out_specs=VMEM,
        scratch_shapes=[pltpu.VMEM(block.shape, jnp.float32)],
        compiler_params=pltpu.CompilerParams(vmem_limit_bytes=8 << 20),
        cost_estimate=pl.CostEstimate(
            flops=4 * size**3, bytes_accessed=4 * block.size * 2, transcendentals=0
        ),
        name="graft",
    )(near(block), near(left_root), near(right_root))


def pick_kernel(take_ref, rows_ref, out_ref, wide_ref, sems):
    chunks = sems.shape[0]
    count, strip, width = wide_ref.shape[0] // chunks, *wide_ref.shape[1:]
    copies = []
    for chunk in range(chunks):
        blocks = pl.ds(chunk * count, count)
        picked = jnp.dot(
            take_ref[pl.ds(chunk * count * strip, count * strip), :],
            rows_ref[...],
            preferred_element_type=jnp.float32,
        )
        wide_ref[blocks] = picked.reshape(count, strip, width)
        copy = pltpu.make_async_copy(wide_ref.at[blocks], out_ref.at[blocks], sems.at[chunk])
        copy.start()
        copies.append(copy)
    for copy in copies:
        copy.wait()


def pick(take, rows, strip):
    width = rows.shape[1]
    shape = (take.shape[0] // strip, strip, width)
    return pl.pallas_call(
        pick_kernel,
        out_shape=jax.ShapeDtypeStruct(shape, jnp.float32),
        in_specs=[VMEM, VMEM],
        out_specs=pl.BlockSpec(memory_space=pltpu.HBM),
        scratch_shapes=[pltpu.VMEM(shape, jnp.float32), pltpu.SemaphoreType.DMA((3,))],
        compiler_params=pltpu.CompilerParams(vmem_limit_bytes=8 << 20),
        cost_estimate=pl.CostEstimate(flops=0, bytes_accessed=1_300_000, transcendentals=0),
        name="pick",
    )(near(take), near(rows))


def local(grads, slot_of, left_stats, right_stats, left_roots, right_roots):
    replicas, owners = lax.axis_size("rep"), lax.axis_size("own")
    strip, width = grads.shape[2:]
    chosen = selections(slot_of, owners, strip)
    downs, ups, own, last, (put, take) = chains(grads[0], replicas, chosen)
    block_size = strip * owners

    near_down, near_up = downs[1], ups[0]
    last, near_down = ordered(last, near_down)
    wide_last = widen(own, near_down, 1)
    wide_last, near_up = ordered(wide_last, near_up)
    wide_first = widen(own, near_up, 0)
    wide_first, far_down = ordered(wide_first, downs[0])
    first = place(put, wide_first, far_down)
    sends = place(put, wide_last, ups[1], first).reshape(owners, strip, width)
    block = lax.all_to_all(sends, "own", 0, 0, tiled=True).reshape(block_size, width)

    grafted = graft(block, left_roots[0, 0], right_roots[0, 0]).reshape(owners, strip, width)
    rows = lax.all_to_all(grafted, "own", 0, 0, tiled=True)

    gram_left = jnp.einsum("ik,jk->ij", block, block, preferred_element_type=jnp.float32)
    gram_right = jnp.einsum("ki,kj->ij", block, block, preferred_element_type=jnp.float32)
    left_next = DECAY * left_stats[0, 0] + (1.0 - DECAY) * gram_left
    right_next = DECAY * right_stats[0, 0] + (1.0 - DECAY) * gram_right

    update = pick(take, rows.reshape(block_size, width), strip)
    return left_next[None, None], right_next[None, None], update


def solution(mesh):
    return jax.shard_map(
        local,
        mesh=mesh,
        in_specs=(
            P("rep", None, "own", None),
            P("rep"),
            P("rep", "own", None, None),
            P("rep", "own", None, None),
            P("rep", "own", None, None),
            P("rep", "own", None, None),
        ),
        out_specs=(P("rep", "own", None, None), P("rep", "own", None, None), P("rep", "own", None)),
        check_vma=False,
    )
```

```python
import functools

import jax
import jax.numpy as jnp
from jax import lax
from jax.experimental import pallas as pl
from jax.experimental.pallas import tpu as pltpu
from jax.sharding import PartitionSpec as P

DECAY = 0.99
EPSILON = 1e-06
PARTS = 2
WAIT_BYTES = 20_000_000
VMEM = pl.BlockSpec(memory_space=pltpu.VMEM)


def near(array):
    return pltpu.with_memory_space_constraint(array, pltpu.VMEM)


def ordered(first, second):
    return lax.optimization_barrier((first, second))


def half_of(width, parity):
    part = lax.rem(lax.axis_index("rep") + parity, 2)
    return pl.ds(pl.multiple_of(part * width, width), width)


def slice_kernel(groups_ref, one_ref, two_ref, sems, *, picks):
    me, replicas = lax.axis_index("rep"), groups_ref.shape[0]
    toward = 1 - 2 * lax.rem(me, 2)
    copies = []
    for at, (out_ref, (ahead, parity)) in enumerate(zip((one_ref, two_ref), picks)):
        group = lax.rem(me + toward * ahead + replicas, replicas)
        source = groups_ref.at[group, :, :, half_of(out_ref.shape[2], parity)]
        copies.append(pltpu.make_async_copy(source, out_ref, sems.at[at]))
    for copy in copies:
        copy.start()
    for copy in copies:
        copy.wait()


def slices(groups, picks):
    shape = groups.shape[1:3] + (groups.shape[3] // PARTS,)
    return pl.pallas_call(
        functools.partial(slice_kernel, picks=picks),
        out_shape=[jax.ShapeDtypeStruct(shape, groups.dtype)] * 2,
        in_specs=[pl.BlockSpec(memory_space=pltpu.HBM)],
        out_specs=[VMEM] * 2,
        scratch_shapes=[pltpu.SemaphoreType.DMA((2,))],
        compiler_params=pltpu.CompilerParams(vmem_limit_bytes=4 << 20),
        cost_estimate=pl.CostEstimate(flops=0, bytes_accessed=1_000_000, transcendentals=0),
        name="slices",
    )(pltpu.with_memory_space_constraint(groups, pltpu.HBM))


def add_kernel(got_ref, own_ref, out_ref, *, first, part):
    columns = half_of(out_ref.shape[2], part)
    blocks, got = out_ref.shape[0], got_ref.shape[0]
    if first > 0:
        out_ref[pl.ds(0, first)] = own_ref[pl.ds(0, first), :, columns]
    rows = pl.ds(first, got)
    out_ref[rows] = got_ref[...] + own_ref[rows, :, columns]
    rest = blocks - first - got
    if rest > 0:
        rows = pl.ds(first + got, rest)
        out_ref[rows] = own_ref[rows, :, columns]


def add(got, own, first, part):
    shape = own.shape[:2] + got.shape[2:]
    return pl.pallas_call(
        functools.partial(add_kernel, first=first, part=part),
        out_shape=jax.ShapeDtypeStruct(shape, got.dtype),
        in_specs=[VMEM] * 2,
        out_specs=VMEM,
        compiler_params=pltpu.CompilerParams(vmem_limit_bytes=4 << 20),
        cost_estimate=pl.CostEstimate(flops=0, bytes_accessed=WAIT_BYTES, transcendentals=0),
        name="add",
    )(near(got), near(own))


def chains(grads, replicas, chosen):
    me = lax.axis_index("rep")
    toward = 1 - 2 * (me % 2)
    reach = replicas // 2
    groups = grads.reshape((replicas, -1) + grads.shape[1:])
    partner = [(i, i + 1 if i % 2 == 0 else i - 1) for i in range(replicas)]
    other = [(i, (i - 1 if i % 2 == 0 else i + 1) % replicas) for i in range(replicas)]

    def mine(ahead):
        return lax.dynamic_index_in_dim(groups, (me + toward * ahead + replicas) % replicas, 0, False)

    one, two = slices(groups, ((reach, 1), (reach, 0)))
    far = [lax.ppermute(one, "rep", partner), lax.ppermute(two, "rep", other)]
    one, groups = ordered(one, groups)
    one, two = slices(groups, ((reach - 1, 0), (1 - reach, 1)))
    near_by = [lax.ppermute(one, "rep", partner), lax.ppermute(two, "rep", other)]
    one, groups = ordered(one, groups)
    last = None
    for step in range(reach - 1, 0, -1):
        for array, at, flip in ((far, step, 0), (near_by, step - 1, 1)):
            if at == 0:
                continue
            passed = [None, None]
            for side, ahead, pairs in ((0, -at, other), (1, at, partner)):
                got = array[side]
                if last is not None:
                    last, got = ordered(last, got)
                if step == reach - 2 and not at == step:
                    chosen, got = ordered(chosen, got)
                last = add(got, mine(ahead), 0, (side + flip) % 2)
                passed[1 - side] = lax.ppermute(last, "rep", pairs)
            array[:] = passed
    return far, near_by, mine(0), last, chosen


def widen_kernel(own_ref, down_ref, out_ref, *, part):
    columns = half_of(out_ref.shape[2], part)
    out_ref[...] = down_ref[...].astype(jnp.float32) + own_ref[:, :, columns].astype(jnp.float32)


def widen(own, down, part):
    return pl.pallas_call(
        functools.partial(widen_kernel, part=part),
        out_shape=jax.ShapeDtypeStruct(down.shape, jnp.float32),
        in_specs=[VMEM] * 2,
        out_specs=VMEM,
        compiler_params=pltpu.CompilerParams(vmem_limit_bytes=4 << 20),
        cost_estimate=pl.CostEstimate(flops=0, bytes_accessed=WAIT_BYTES, transcendentals=0),
        name="widen",
    )(near(own), near(down))


def selections(slot_of, owners, strip):
    slot = jnp.repeat(slot_of, strip)
    blocks, slots = jnp.arange(slot.shape[0]), jnp.arange(owners * strip)
    same_row = blocks[None, :] % strip == slots[:, None] % strip
    put = (slot[None, :] == slots[:, None] // strip) & same_row
    take = (slot[:, None] == slots[None, :] // strip) & (
        blocks[:, None] % strip == slots[None, :] % strip
    )
    return put.astype(jnp.bfloat16), take.astype(jnp.bfloat16)


def put_kernel(put_ref, wide_ref, got_ref, out_ref):
    total = (wide_ref[...] + got_ref[...].astype(jnp.float32)).astype(out_ref.dtype)
    out_ref[...] = jnp.dot(
        put_ref[...], total.reshape(-1, total.shape[2]), preferred_element_type=jnp.float32
    ).astype(out_ref.dtype)


def place_kernel(put_ref, wide_ref, got_ref, before_ref, out_ref):
    width = got_ref.shape[2]
    total = (wide_ref[...] + got_ref[...].astype(jnp.float32)).astype(out_ref.dtype)
    out_ref[:, half_of(width, 1)] = before_ref[...]
    out_ref[:, half_of(width, 0)] = jnp.dot(
        put_ref[...], total.reshape(-1, width), preferred_element_type=jnp.float32
    ).astype(out_ref.dtype)


def place(put, wide, got, *before):
    width = got.shape[2]
    columns = width + sum(a.shape[1] for a in before)
    return pl.pallas_call(
        place_kernel if before else put_kernel,
        out_shape=jax.ShapeDtypeStruct((put.shape[0], columns), got.dtype),
        in_specs=[VMEM] * (3 + len(before)),
        out_specs=VMEM,
        compiler_params=pltpu.CompilerParams(vmem_limit_bytes=8 << 20),
        cost_estimate=pl.CostEstimate(flops=0, bytes_accessed=WAIT_BYTES, transcendentals=0),
        name="place",
    )(*[near(a) for a in (put, wide, got) + before])


def step_kernel(block_ref, left_ref, right_ref, out_ref, precond_ref):
    size = block_ref.shape[0]
    tile = size
    block = block_ref[...]
    squares = jnp.zeros((tile, size), jnp.float32)
    inputs = jnp.zeros((tile, size), jnp.float32)
    for i in range(1):
        rows = pl.ds(i * tile, tile)
        wide = block_ref[rows, :].astype(jnp.float32)
        inputs += wide * wide
        half = jnp.dot(left_ref[rows, :], block, preferred_element_type=jnp.float32)
        precond = jnp.dot(
            half.astype(jnp.bfloat16), right_ref[...], preferred_element_type=jnp.float32
        )
        precond_ref[rows, :] = precond
        squares += precond * precond
    count = 1.0 / (size * size)
    ratio = jnp.sqrt(jnp.sum(inputs, keepdims=True) * count + EPSILON) / jnp.sqrt(
        jnp.sum(squares, keepdims=True) * count + EPSILON
    )
    for i in range(1):
        rows = pl.ds(i * tile, tile)
        out_ref[rows, :] = (precond_ref[rows, :] * ratio).astype(out_ref.dtype)


def graft(block, left_root, right_root):
    size = block.shape[0]
    return pl.pallas_call(
        step_kernel,
        out_shape=jax.ShapeDtypeStruct(block.shape, block.dtype),
        in_specs=[VMEM] * 3,
        out_specs=VMEM,
        scratch_shapes=[pltpu.VMEM(block.shape, jnp.float32)],
        compiler_params=pltpu.CompilerParams(vmem_limit_bytes=8 << 20),
        cost_estimate=pl.CostEstimate(
            flops=4 * size**3, bytes_accessed=4 * block.size * 2, transcendentals=0
        ),
        name="graft",
    )(near(block), near(left_root), near(right_root))


def pick_kernel(take_ref, rows_ref, out_ref, wide_ref, sems):
    chunks = sems.shape[0]
    count, strip, width = wide_ref.shape[0] // chunks, *wide_ref.shape[1:]
    copies = []
    for chunk in range(chunks):
        blocks = pl.ds(chunk * count, count)
        picked = jnp.dot(
            take_ref[pl.ds(chunk * count * strip, count * strip), :],
            rows_ref[...],
            preferred_element_type=jnp.float32,
        )
        wide_ref[blocks] = picked.reshape(count, strip, width)
        copy = pltpu.make_async_copy(wide_ref.at[blocks], out_ref.at[blocks], sems.at[chunk])
        copy.start()
        copies.append(copy)
    for copy in copies:
        copy.wait()


def pick(take, rows, strip):
    width = rows.shape[1]
    shape = (take.shape[0] // strip, strip, width)
    return pl.pallas_call(
        pick_kernel,
        out_shape=jax.ShapeDtypeStruct(shape, jnp.float32),
        in_specs=[VMEM, VMEM],
        out_specs=pl.BlockSpec(memory_space=pltpu.HBM),
        scratch_shapes=[pltpu.VMEM(shape, jnp.float32), pltpu.SemaphoreType.DMA((3,))],
        compiler_params=pltpu.CompilerParams(vmem_limit_bytes=8 << 20),
        cost_estimate=pl.CostEstimate(flops=0, bytes_accessed=1_300_000, transcendentals=0),
        name="pick",
    )(near(take), near(rows))


def local(grads, slot_of, left_stats, right_stats, left_roots, right_roots):
    replicas, owners = lax.axis_size("rep"), lax.axis_size("own")
    strip, width = grads.shape[2:]
    chosen = selections(slot_of, owners, strip)
    far, near_by, own, last, (put, take) = chains(grads[0], replicas, chosen)
    block_size = strip * owners

    last, near_two = ordered(last, near_by[1])
    wide_first = widen(own, near_two, 0)
    wide_first, near_one = ordered(wide_first, near_by[0])
    wide_last = widen(own, near_one, 1)
    wide_last, far_two = ordered(wide_last, far[1])
    first = place(put, wide_last, far_two)
    sends = place(put, wide_first, far[0], first).reshape(owners, strip, width)
    block = lax.all_to_all(sends, "own", 0, 0, tiled=True).reshape(block_size, width)

    grafted = graft(block, left_roots[0, 0], right_roots[0, 0]).reshape(owners, strip, width)
    rows = lax.all_to_all(grafted, "own", 0, 0, tiled=True)

    gram_left = jnp.einsum("ik,jk->ij", block, block, preferred_element_type=jnp.float32)
    gram_right = jnp.einsum("ki,kj->ij", block, block, preferred_element_type=jnp.float32)
    left_next = DECAY * left_stats[0, 0] + (1.0 - DECAY) * gram_left
    right_next = DECAY * right_stats[0, 0] + (1.0 - DECAY) * gram_right

    update = pick(take, rows.reshape(block_size, width), strip)
    return left_next[None, None], right_next[None, None], update


def solution(mesh):
    return jax.shard_map(
        local,
        mesh=mesh,
        in_specs=(
            P("rep", None, "own", None),
            P("rep"),
            P("rep", "own", None, None),
            P("rep", "own", None, None),
            P("rep", "own", None, None),
            P("rep", "own", None, None),
        ),
        out_specs=(P("rep", "own", None, None), P("rep", "own", None, None), P("rep", "own", None)),
        check_vma=False,
    )
```

```python
import functools

import jax
import jax.numpy as jnp
from jax import lax
from jax.experimental import pallas as pl
from jax.experimental.pallas import tpu as pltpu
from jax.sharding import PartitionSpec as P

DECAY = 0.99
EPSILON = 1e-06
PARTS = 2
WAIT_BYTES = 20_000_000
VMEM = pl.BlockSpec(memory_space=pltpu.VMEM)


def near(array):
    return pltpu.with_memory_space_constraint(array, pltpu.VMEM)


def ordered(first, second):
    return lax.optimization_barrier((first, second))


def slice_kernel(groups_ref, one_ref, two_ref, sems, *, picks):
    me = lax.axis_index("rep")
    width = one_ref.shape[2]
    copies = []
    for at, (out_ref, (ahead, part)) in enumerate(zip((one_ref, two_ref), picks)):
        group = lax.rem(me + ahead, groups_ref.shape[0])
        source = groups_ref.at[group, :, :, pl.ds(part * width, width)]
        copies.append(pltpu.make_async_copy(source, out_ref, sems.at[at]))
    for copy in copies:
        copy.start()
    for copy in copies:
        copy.wait()


def slices(groups, picks):
    shape = groups.shape[1:3] + (groups.shape[3] // PARTS,)
    return pl.pallas_call(
        functools.partial(slice_kernel, picks=picks),
        out_shape=[jax.ShapeDtypeStruct(shape, groups.dtype)] * 2,
        in_specs=[pl.BlockSpec(memory_space=pltpu.HBM)],
        out_specs=[VMEM] * 2,
        scratch_shapes=[pltpu.SemaphoreType.DMA((2,))],
        compiler_params=pltpu.CompilerParams(vmem_limit_bytes=4 << 20),
        cost_estimate=pl.CostEstimate(flops=0, bytes_accessed=1_000_000, transcendentals=0),
        name="slices",
    )(pltpu.with_memory_space_constraint(groups, pltpu.HBM))


def add_kernel(got_ref, own_ref, out_ref, *, first, part):
    width = out_ref.shape[2]
    columns = pl.ds(part * width, width)
    blocks, got = out_ref.shape[0], got_ref.shape[0]
    if first > 0:
        out_ref[pl.ds(0, first)] = own_ref[pl.ds(0, first), :, columns]
    rows = pl.ds(first, got)
    out_ref[rows] = got_ref[...] + own_ref[rows, :, columns]
    rest = blocks - first - got
    if rest > 0:
        rows = pl.ds(first + got, rest)
        out_ref[rows] = own_ref[rows, :, columns]


def add(got, own, first, part):
    shape = own.shape[:2] + got.shape[2:]
    return pl.pallas_call(
        functools.partial(add_kernel, first=first, part=part),
        out_shape=jax.ShapeDtypeStruct(shape, got.dtype),
        in_specs=[VMEM] * 2,
        out_specs=VMEM,
        compiler_params=pltpu.CompilerParams(vmem_limit_bytes=4 << 20),
        cost_estimate=pl.CostEstimate(flops=0, bytes_accessed=WAIT_BYTES, transcendentals=0),
        name="add",
    )(near(got), near(own))


def chains(grads, replicas, chosen):
    me = lax.axis_index("rep")
    reach = replicas // 2
    groups = grads.reshape((replicas, -1) + grads.shape[1:])
    ahead = [(i, (i - 1) % replicas) for i in range(replicas)]
    back = [(i, (i + 1) % replicas) for i in range(replicas)]

    def mine(group):
        return lax.dynamic_index_in_dim(groups, (group + replicas) % replicas, 0, False)

    down, up = [None, None], [None, None]
    one, two = slices(groups, ((reach, 0), (reach, 1)))
    down[0], up[1] = lax.ppermute(one, "rep", back), lax.ppermute(two, "rep", ahead)
    one, groups = ordered(one, groups)
    one, two = slices(groups, ((reach - 1, 1), (reach + 1, 0)))
    down[1], up[0] = lax.ppermute(one, "rep", back), lax.ppermute(two, "rep", ahead)
    one, groups = ordered(one, groups)
    last = None
    for step in range(reach - 1, 0, -1):
        for at, one, two in ((step, 0, 1), (step - 1, 1, 0)):
            if at == 0:
                continue
            sends = [(down, one, me + at, back), (up, two, me - at, ahead)]
            for array, part, group, pairs in sends[::-1] if step == 1 else sends:
                got = array[part]
                if last is not None:
                    last, got = ordered(last, got)
                if step == reach - 2 and not at == step:
                    chosen, got = ordered(chosen, got)
                last = add(got, mine(group), 0, part)
                array[part] = lax.ppermute(last, "rep", pairs)
    return down, up, mine(me), last, chosen


def widen_kernel(own_ref, down_ref, out_ref, *, part):
    width = out_ref.shape[2]
    columns = pl.ds(part * width, width)
    out_ref[...] = down_ref[...].astype(jnp.float32) + own_ref[:, :, columns].astype(jnp.float32)


def widen(own, down, part):
    return pl.pallas_call(
        functools.partial(widen_kernel, part=part),
        out_shape=jax.ShapeDtypeStruct(down.shape, jnp.float32),
        in_specs=[VMEM] * 2,
        out_specs=VMEM,
        compiler_params=pltpu.CompilerParams(vmem_limit_bytes=4 << 20),
        cost_estimate=pl.CostEstimate(flops=0, bytes_accessed=WAIT_BYTES, transcendentals=0),
        name="widen",
    )(near(own), near(down))


def selections(slot_of, owners, strip):
    slot = jnp.repeat(slot_of, strip)
    blocks, slots = jnp.arange(slot.shape[0]), jnp.arange(owners * strip)
    same_row = blocks[None, :] % strip == slots[:, None] % strip
    put = (slot[None, :] == slots[:, None] // strip) & same_row
    take = (slot[:, None] == slots[None, :] // strip) & (
        blocks[:, None] % strip == slots[None, :] % strip
    )
    return put.astype(jnp.bfloat16), take.astype(jnp.bfloat16)


def place_kernel(put_ref, wide_ref, got_ref, *refs):
    before, out_ref = refs[:-1], refs[-1]
    width = got_ref.shape[2]
    total = (wide_ref[...] + got_ref[...].astype(jnp.float32)).astype(out_ref.dtype)
    for ref in before:
        out_ref[:, pl.ds(0, ref.shape[1])] = ref[...]
    out_ref[:, pl.ds(out_ref.shape[1] - width, width)] = jnp.dot(
        put_ref[...], total.reshape(-1, width), preferred_element_type=jnp.float32
    ).astype(out_ref.dtype)


def place(put, wide, got, *before):
    width = got.shape[2]
    columns = width + sum(a.shape[1] for a in before)
    return pl.pallas_call(
        place_kernel,
        out_shape=jax.ShapeDtypeStruct((put.shape[0], columns), got.dtype),
        in_specs=[VMEM] * (3 + len(before)),
        out_specs=VMEM,
        compiler_params=pltpu.CompilerParams(vmem_limit_bytes=8 << 20),
        cost_estimate=pl.CostEstimate(flops=0, bytes_accessed=WAIT_BYTES, transcendentals=0),
        name="place",
    )(*[near(a) for a in (put, wide, got) + before])


def step_kernel(block_ref, left_ref, right_ref, out_ref, precond_ref):
    size = block_ref.shape[0]
    tile = size
    block = block_ref[...]
    squares = jnp.zeros((tile, size), jnp.float32)
    inputs = jnp.zeros((tile, size), jnp.float32)
    for i in range(1):
        rows = pl.ds(i * tile, tile)
        wide = block_ref[rows, :].astype(jnp.float32)
        inputs += wide * wide
        half = jnp.dot(left_ref[rows, :], block, preferred_element_type=jnp.float32)
        precond = jnp.dot(
            half.astype(jnp.bfloat16), right_ref[...], preferred_element_type=jnp.float32
        )
        precond_ref[rows, :] = precond
        squares += precond * precond
    count = 1.0 / (size * size)
    ratio = jnp.sqrt(jnp.sum(inputs, keepdims=True) * count + EPSILON) / jnp.sqrt(
        jnp.sum(squares, keepdims=True) * count + EPSILON
    )
    for i in range(1):
        rows = pl.ds(i * tile, tile)
        out_ref[rows, :] = (precond_ref[rows, :] * ratio).astype(out_ref.dtype)


def graft(block, left_root, right_root):
    size = block.shape[0]
    return pl.pallas_call(
        step_kernel,
        out_shape=jax.ShapeDtypeStruct(block.shape, block.dtype),
        in_specs=[VMEM] * 3,
        out_specs=VMEM,
        scratch_shapes=[pltpu.VMEM(block.shape, jnp.float32)],
        compiler_params=pltpu.CompilerParams(vmem_limit_bytes=8 << 20),
        cost_estimate=pl.CostEstimate(
            flops=4 * size**3, bytes_accessed=4 * block.size * 2, transcendentals=0
        ),
        name="graft",
    )(near(block), near(left_root), near(right_root))


def pick_kernel(take_ref, rows_ref, out_ref, wide_ref, sems):
    chunks = sems.shape[0]
    count, strip, width = wide_ref.shape[0] // chunks, *wide_ref.shape[1:]
    copies = []
    for chunk in range(chunks):
        blocks = pl.ds(chunk * count, count)
        picked = jnp.dot(
            take_ref[pl.ds(chunk * count * strip, count * strip), :],
            rows_ref[...],
            preferred_element_type=jnp.float32,
        )
        wide_ref[blocks] = picked.reshape(count, strip, width)
        copy = pltpu.make_async_copy(wide_ref.at[blocks], out_ref.at[blocks], sems.at[chunk])
        copy.start()
        copies.append(copy)
    for copy in copies:
        copy.wait()


def pick(take, rows, strip):
    width = rows.shape[1]
    shape = (take.shape[0] // strip, strip, width)
    return pl.pallas_call(
        pick_kernel,
        out_shape=jax.ShapeDtypeStruct(shape, jnp.float32),
        in_specs=[VMEM, VMEM],
        out_specs=pl.BlockSpec(memory_space=pltpu.HBM),
        scratch_shapes=[pltpu.VMEM(shape, jnp.float32), pltpu.SemaphoreType.DMA((3,))],
        compiler_params=pltpu.CompilerParams(vmem_limit_bytes=8 << 20),
        cost_estimate=pl.CostEstimate(flops=0, bytes_accessed=1_300_000, transcendentals=0),
        name="pick",
    )(near(take), near(rows))


def local(grads, slot_of, left_stats, right_stats, left_roots, right_roots):
    replicas, owners = lax.axis_size("rep"), lax.axis_size("own")
    strip, width = grads.shape[2:]
    chosen = selections(slot_of, owners, strip)
    downs, ups, own, last, (put, take) = chains(grads[0], replicas, chosen)
    block_size = strip * owners

    near_down, near_up = downs[1], ups[0]
    last, near_down = ordered(last, near_down)
    wide_last = widen(own, near_down, 1)
    wide_last, near_up = ordered(wide_last, near_up)
    wide_first = widen(own, near_up, 0)
    wide_first, far_down = ordered(wide_first, downs[0])
    first = place(put, wide_first, far_down)
    sends = place(put, wide_last, ups[1], first).reshape(owners, strip, width)
    block = lax.all_to_all(sends, "own", 0, 0, tiled=True).reshape(block_size, width)

    grafted = graft(block, left_roots[0, 0], right_roots[0, 0]).reshape(owners, strip, width)
    rows = lax.all_to_all(grafted, "own", 0, 0, tiled=True)

    gram_left = jnp.einsum("ik,jk->ij", block, block, preferred_element_type=jnp.float32)
    gram_right = jnp.einsum("ki,kj->ij", block, block, preferred_element_type=jnp.float32)
    left_next = DECAY * left_stats[0, 0] + (1.0 - DECAY) * gram_left
    right_next = DECAY * right_stats[0, 0] + (1.0 - DECAY) * gram_right

    update = pick(take, rows.reshape(block_size, width), strip)
    return left_next[None, None], right_next[None, None], update


def solution(mesh):
    return jax.shard_map(
        local,
        mesh=mesh,
        in_specs=(
            P("rep", None, "own", None),
            P("rep"),
            P("rep", "own", None, None),
            P("rep", "own", None, None),
            P("rep", "own", None, None),
            P("rep", "own", None, None),
        ),
        out_specs=(P("rep", "own", None, None), P("rep", "own", None, None), P("rep", "own", None)),
        check_vma=False,
    )
```
